32 devices in a mesh: row: 8 (over y, x, core), col: 4 (over z).
Axes of the slice: x: 2, y: 2, z: 4, core: 2. Of those that a mesh axis runs over, the one named last changes fastest.
Arguments:
- amplitudes: bfloat16 [1024, 32768], P('row', 'col'), may hold values from -6 to 6
- integrals: bfloat16 [32768, 32768], P('col', 'row'), may hold values from -0.0390625 to 0.0390625
- tile_mask: int32 [256, 256], P('col', 'row'), may hold values 0 or 1
- driving: bfloat16 [1024, 32768], P('col', 'row'), may hold values from -6 to 6
- occupied_energy: float32 [1024], P('col'), may hold values from -1.5 to -0.5
- virtual_energy: float32 [32768], P('row'), may hold values from 0.5 to 2.5
Outputs:
- update: float32 [1024, 32768], P('col', 'row')
The draws below stay inside these ranges and needn't reach their ends.
All inputs are finite; a program needn't handle non-finite values. No bound on the sum of `tile_mask` on one device may be relied on, other than what follows from the above.
Results may differ from the reference program's by a relative error of at most 0.0003.
Values may be sent and summed in bfloat16 or wider, within the bound.
No kernel may reach another device: no remote copies, remote signals or barrier semaphores. Data moves between devices by JAX's collectives and lax.ppermute only.
A program may use at most 256 MiB of HBM per device.

```python
import math
import jax
import jax.numpy as jnp
from jax import lax

VP = 32768
TILE = 128
ROWS = 1024
NT = 256


def with_ends(drawn, rng, smallest, top_value):
    longest = drawn.shape.index(max(drawn.shape))
    spots = []
    for shift in (0, 1):
        where = [jax.random.randint(jax.random.fold_in(rng, axis), (), 0, length) for axis, length in enumerate(drawn.shape)]
        where[longest] = (where[longest] + shift) % drawn.shape[longest]
        spots.append(tuple(where))
    return drawn.at[spots[0]].set(smallest).at[spots[1]].set(top_value)


def steps_of(rng, extent, split, smallest, top_value):
    level, own = 1.0, jax.random.fold_in(rng, 6)
    for axis_at, shards_of in split:
        steps = jnp.exp(jax.random.uniform(jax.random.fold_in(own, axis_at), (shards_of,), jnp.float32, smallest / len(split), top_value / len(split)))
        level = level * jnp.repeat(steps, extent[axis_at] // shards_of).reshape([-1 if axis == axis_at else 1 for axis in range(len(extent))])
    return level


def scatter_about(own_key, shape, scale, reach, pieces=(), held_as=jnp.bfloat16):
    drawn = scale * jax.random.normal(own_key, shape, jnp.float32)
    if pieces:
        drawn = drawn * steps_of(own_key, shape, pieces, -0.22, 0.18)
    return jnp.clip(drawn, -reach, reach).astype(held_as)


def setup_inputs(seed: int = 0) -> dict:
    splits = jax.random.split(jax.random.key(seed), 7)
    amplitudes = scatter_about(splits[0], (ROWS, VP), 1.0, 6.0, ((0, 8), (1, 4)))
    integrals = scatter_about(splits[1], (VP, VP), (3 * VP // 5) ** -0.5, 0.0390625, ((0, 4), (1, 8)))
    tile_mask = with_ends((jax.random.randint(splits[2], (NT, NT), 0, 5) < 3).astype(jnp.int32), jax.random.fold_in(splits[2], 1), 0, 1)
    driving = scatter_about(splits[3], (ROWS, VP), 1.0, 6.0, ((0, 4), (1, 8)))
    occupied_energy = jnp.clip(-1.5 + 1.0 * jax.random.uniform(splits[4], (ROWS,), jnp.float32) ** steps_of(splits[4], (ROWS,), ((0, 4),), -0.2, 0.2), -1.5, -0.5)
    virtual_energy = jnp.clip(jnp.exp(math.log(2.5) - 1.609438 * jax.random.uniform(splits[5], (VP,), jnp.float32) ** steps_of(splits[5], (VP,), ((0, 8),), -0.2, 0.2)), 0.5, 2.5)
    return dict(amplitudes=amplitudes, integrals=integrals, tile_mask=tile_mask, driving=driving, occupied_energy=occupied_energy, virtual_energy=virtual_energy)


def reference(amplitudes, integrals, tile_mask, driving, occupied_energy, virtual_energy):
    width = 16 * TILE
    blocks = VP // width
    mask_vals = tile_mask.astype(jnp.bfloat16)

    def one_block(index):
        start = (index * width).astype(jnp.int32)
        columns = lax.dynamic_slice_in_dim(integrals, start, width, 1)
        tiles = lax.dynamic_slice_in_dim(mask_vals, (index * 16).astype(jnp.int32), 16, 1)
        shaped = columns.reshape(NT, TILE, 16, TILE) * tiles[:, None, :, None]
        masked = shaped.reshape(VP, width)
        return jnp.dot(amplitudes, masked, preferred_element_type=jnp.float32)

    parts = lax.map(one_block, jnp.arange(blocks, dtype=jnp.int32))
    ladder = jnp.transpose(parts, (1, 0, 2)).reshape(ROWS, VP)
    denom = virtual_energy[None, :] - occupied_energy[:, None]
    return (driving.astype(jnp.float32) + ladder) / denom
```

```python
import functools
import jax
import jax.numpy as jnp
from jax import lax
from jax.experimental import pallas as pl
from jax.experimental.pallas import tpu as pltpu
from jax.sharding import PartitionSpec as P

MIB = 2**20


def product_kernel(pieces, waits, slot_ref, *refs):
    sources = refs[: len(pieces)]
    integrals_ref, mask_ref, out_ref, rows, masked, sems = refs[len(pieces) + waits :]

    @pl.when(pl.program_id(0) == 0)
    def _():
        copies = []
        for ref, count in zip(sources, pieces):
            for k in range(count):
                g = len(copies)
                source = ref.at[k] if count > 1 else ref
                copies.append(pltpu.make_async_copy(source, rows.at[slot_ref[g]], sems.at[g]))
        for copy in copies:
            copy.start()
        for copy in copies:
            copy.wait()

    tile = masked.shape[0] // mask_ref.shape[0]
    for t in range(mask_ref.shape[0]):
        part = slice(t * tile, (t + 1) * tile)
        masked[part, :] = integrals_ref[part, :] * mask_ref[t : t + 1, :]
    every = rows[...].reshape(rows.shape[0] * rows.shape[1], rows.shape[2])
    total = jnp.dot(every, masked[...], preferred_element_type=jnp.float32)
    out_ref[...] = total.reshape(out_ref.shape)


def product(arrays, slots, integrals, mask, first, width, block, waits):
    m, depth = arrays[0].shape[-2:]
    pieces = [a.shape[0] if a.ndim == 3 else 1 for a in arrays]
    devices, tiles = sum(pieces), mask.shape[0]
    grid_spec = pltpu.PrefetchScalarGridSpec(
        num_scalar_prefetch=1,
        grid=(width // block,),
        in_specs=[pl.BlockSpec(memory_space=pl.ANY)] * (len(arrays) + len(waits))
        + [
            pl.BlockSpec((depth, block), lambda n, s: (0, first // block + n)),
            pl.BlockSpec((tiles, block), lambda n, s: (0, first // block + n)),
        ],
        out_specs=pl.BlockSpec((devices, m, block), lambda n, s: (0, 0, n)),
        scratch_shapes=[
            pltpu.VMEM((devices, m, depth), jnp.bfloat16),
            pltpu.VMEM((depth, block), jnp.bfloat16),
            pltpu.SemaphoreType.DMA((devices,)),
        ],
    )
    return pl.pallas_call(
        functools.partial(product_kernel, pieces, len(waits)),
        grid_spec=grid_spec,
        out_shape=jax.ShapeDtypeStruct((devices, m, width), jnp.float32),
        compiler_params=pltpu.CompilerParams(vmem_limit_bytes=56 * MIB),
        cost_estimate=pl.CostEstimate(
            flops=2 * devices * m * depth * width,
            bytes_accessed=2 * depth * width + 4 * devices * m * width,
            transcendentals=0,
        ),
    )(slots, *arrays, *waits, integrals, mask)


def gather(own, rows):
    swap = [(i, i ^ 1) for i in range(rows)]
    others = [lax.ppermute(own, "row", [(i, i ^ q) for i in range(rows)]) for q in range(2, rows, 2)]
    pieces = [own, lax.ppermute(own, "row", swap)]
    for other in others:
        pieces += [other, lax.ppermute(other, "row", swap)]
    return pieces


def send(values, cols, edge):
    pairs = [(edge, edge + 1), (cols - 1 - edge, cols - 2 - edge)]
    return lax.ppermute(values, "col", pairs)


def after(value, others):
    return lax.optimization_barrier((value, *others))[0]


class Chain:
    def __init__(self, sums, cols, split):
        self.sums, self.cols, self.last = sums, cols, cols - 1
        self.groups = [(s, s + 1) for s in range(cols - 1)] if split else [(0, cols - 1)]
        self.came, self.ends = {}, []

    def advance(self, edge, order):
        last, came = self.last, {}
        for low, high in self.groups:
            at = max(low, edge)
            if at >= high:
                continue
            if edge < self.cols // 2:
                values = self.sums[at:high]
            else:
                values = jnp.flip(self.sums[last - high : last - at], 0)
            if edge:
                first, received = self.came[at - 1]
                received = after(received, order)
                values = values + received[at - 1 - first : high - 1 - first].astype(jnp.float32)
            values = values.astype(jnp.float16)
            order = [values]
            received = send(values, self.cols, edge)
            for k in range(at, high):
                came[k] = (at, received)
        self.came = came
        self.ends.append(received)
        return order

    def total(self):
        total = self.sums[self.last]
        for received in self.ends:
            total = total + received[-1].astype(jnp.float32)
        return total


def plan(local):
    if local == 128:
        return ((32, False, 1), (32, True, 1), (64, True, 2))
    return ((local, True, 1),)


def shards(rows, cols, amplitudes, integrals, tile_mask, driving, occupied_energy, virtual_energy):
    local, depth = amplitudes.shape
    width = integrals.shape[1]
    share = rows // cols
    me, place = lax.axis_index("row"), lax.axis_index("col")
    mask = jnp.repeat(tile_mask.astype(jnp.bfloat16), width // tile_mask.shape[1], axis=1)

    lower = place < cols // 2
    near = jnp.where(lower, place, cols - 1 - place)

    def slot_of(device):
        target = device // share
        target = jnp.where(lower, target, cols - 1 - target)
        return jnp.remainder(2 * cols - 1 + near - target, cols) * share + device % share

    device = jnp.arange(rows, dtype=jnp.int32)
    slots_all, slots_xor = slot_of(device), slot_of(jnp.bitwise_xor(device, me))

    driving = driving.reshape(share, local, width)
    occupied = occupied_energy.reshape(share, local, 1)
    layout = plan(local)
    count = sum(chunks for _, _, chunks in layout)
    chains, order, begun, offset, where = [], [], [], 0, []
    for m, whole, chunks in layout:
        part = slice(offset, offset + m)
        offset += m
        own = after(amplitudes[part], begun)
        if whole:
            arrays, slots = [lax.all_gather(own, "row", axis=0)], slots_all
        else:
            arrays, slots = gather(own, rows), slots_xor
            begun = arrays[2::2]
        chunk = width // chunks
        for c in range(chunks):
            at = c * chunk
            sums = product(arrays, after(slots, order), integrals, mask, at, chunk, min(chunk, 512), [])
            split = cols == 4 and len(chains) == count - 1
            chains.append(Chain(sums.reshape(cols, share, m, chunk), cols, split))
            where.append((part, slice(at, at + chunk)))
            for edge, chain in enumerate(chains[: -cols : -1]):
                order = chain.advance(edge, order)
    for late in range(1, cols - 1):
        for edge in range(late, cols - 1):
            if edge - late < len(chains):
                order = chains[late - edge - 1].advance(edge, order)

    outs = {}
    for (part, span), chain in zip(where, chains):
        denom = virtual_energy[None, None, span] - occupied[:, part]
        value = (driving[:, part, span].astype(jnp.float32) + chain.total()) / denom
        outs.setdefault(part.start, []).append(value)
    outs = [jnp.concatenate(parts, axis=2) for parts in outs.values()]
    return jnp.concatenate(outs, axis=1).reshape(share * local, width)


def solution(mesh):
    in_specs = (
        P("row", "col"),
        P("col", "row"),
        P("col", "row"),
        P("col", "row"),
        P("col"),
        P("row"),
    )
    fn = functools.partial(shards, mesh.shape["row"], mesh.shape["col"])
    return jax.shard_map(fn, mesh=mesh, in_specs=in_specs, out_specs=P("col", "row"), check_vma=False)
```

```python
import functools
import jax
import jax.numpy as jnp
from jax import lax
from jax.experimental import pallas as pl
from jax.experimental.pallas import tpu as pltpu
from jax.sharding import PartitionSpec as P

MIB = 2**20


def product_kernel(pieces, slot_ref, *refs):
    sources = refs[: len(pieces)]
    integrals_ref, mask_ref, out_ref, rows, masked, sems = refs[len(pieces) :]

    @pl.when(pl.program_id(0) == 0)
    def _():
        copies = []
        for ref, count in zip(sources, pieces):
            for k in range(count):
                g = len(copies)
                source = ref.at[k] if count > 1 else ref
                copies.append(pltpu.make_async_copy(source, rows.at[slot_ref[g]], sems.at[g]))
        for copy in copies:
            copy.start()
        for copy in copies:
            copy.wait()

    tile = masked.shape[0] // mask_ref.shape[0]
    for t in range(mask_ref.shape[0]):
        part = slice(t * tile, (t + 1) * tile)
        masked[part, :] = integrals_ref[part, :] * mask_ref[t : t + 1, :]
    every = rows[...].reshape(rows.shape[0] * rows.shape[1], rows.shape[2])
    total = jnp.dot(every, masked[...], preferred_element_type=jnp.float32)
    out_ref[...] = total.reshape(out_ref.shape)


def product(arrays, slots, integrals, mask, first, width, block):
    m, depth = arrays[0].shape[-2:]
    pieces = [a.shape[0] if a.ndim == 3 else 1 for a in arrays]
    devices, tiles = sum(pieces), mask.shape[0]
    grid_spec = pltpu.PrefetchScalarGridSpec(
        num_scalar_prefetch=1,
        grid=(width // block,),
        in_specs=[pl.BlockSpec(memory_space=pl.ANY)] * len(arrays)
        + [
            pl.BlockSpec((depth, block), lambda n, s: (0, first // block + n)),
            pl.BlockSpec((tiles, block), lambda n, s: (0, first // block + n)),
        ],
        out_specs=pl.BlockSpec((devices, m, block), lambda n, s: (0, 0, n)),
        scratch_shapes=[
            pltpu.VMEM((devices, m, depth), jnp.bfloat16),
            pltpu.VMEM((depth, block), jnp.bfloat16),
            pltpu.SemaphoreType.DMA((devices,)),
        ],
    )
    return pl.pallas_call(
        functools.partial(product_kernel, pieces),
        grid_spec=grid_spec,
        out_shape=jax.ShapeDtypeStruct((devices, m, width), jnp.float32),
        compiler_params=pltpu.CompilerParams(vmem_limit_bytes=56 * MIB),
        cost_estimate=pl.CostEstimate(
            flops=2 * devices * m * depth * width,
            bytes_accessed=2 * depth * width + 4 * devices * m * width,
            transcendentals=0,
        ),
    )(slots, *arrays, integrals, mask)


def gather(own, rows):
    swap = [(i, i ^ 1) for i in range(rows)]
    pieces = [own, lax.ppermute(own, "row", swap)]
    for q in range(2, rows, 2):
        other = lax.ppermute(own, "row", [(i, i ^ q) for i in range(rows)])
        other = after(other, pieces[1:2])
        pieces += [other, lax.ppermute(other, "row", swap)]
    return pieces


def send(values, cols, edge):
    pairs = [(edge, edge + 1), (cols - 1 - edge, cols - 2 - edge)]
    return lax.ppermute(values, "col", pairs)


def after(value, others):
    return lax.optimization_barrier((value, *others))[0]


class Chain:
    def __init__(self, sums, cols, split):
        self.sums, self.cols, self.last = sums, cols, cols - 1
        self.groups = [(s, s + 1) for s in range(cols - 1)] if split else [(0, cols - 1)]
        self.came, self.ends = {}, []

    def advance(self, edge, order):
        last, came = self.last, {}
        for low, high in self.groups:
            at = max(low, edge)
            if at >= high:
                continue
            if edge < self.cols // 2:
                values = self.sums[at:high]
            else:
                values = jnp.flip(self.sums[last - high : last - at], 0)
            if edge:
                first, received = self.came[at - 1]
                received = after(received, order)
                values = values + received[at - 1 - first : high - 1 - first].astype(jnp.float32)
            values = values.astype(jnp.float16)
            order = [values]
            received = send(values, self.cols, edge)
            for k in range(at, high):
                came[k] = (at, received)
        self.came = came
        self.ends.append(received)
        return order

    def total(self):
        total = self.sums[self.last]
        for received in self.ends:
            total = total + received[-1].astype(jnp.float32)
        return total


def plan(local):
    if local == 128:
        return ((16, False, (8,)), (48, True, (8,)), (64, True, (4, 4)))
    return ((local, True, (8,)),)


def shards(rows, cols, amplitudes, integrals, tile_mask, driving, occupied_energy, virtual_energy):
    local, depth = amplitudes.shape
    width = integrals.shape[1]
    share = rows // cols
    me, place = lax.axis_index("row"), lax.axis_index("col")
    mask = jnp.repeat(tile_mask.astype(jnp.bfloat16), width // tile_mask.shape[1], axis=1)

    lower = place < cols // 2
    near = jnp.where(lower, place, cols - 1 - place)

    def slot_of(device):
        target = device // share
        target = jnp.where(lower, target, cols - 1 - target)
        return jnp.remainder(2 * cols - 1 + near - target, cols) * share + device % share

    device = jnp.arange(rows, dtype=jnp.int32)
    slots_all, slots_xor = slot_of(device), slot_of(jnp.bitwise_xor(device, me))

    driving = driving.reshape(share, local, width)
    occupied = occupied_energy.reshape(share, local, 1)
    layout = plan(local)
    count = sum(len(chunks) for _, _, chunks in layout)
    chains, order, offset, where = [], [], 0, []
    for m, whole, chunks in layout:
        part = slice(offset, offset + m)
        offset += m
        own = amplitudes[part]
        if whole:
            arrays, slots = [lax.all_gather(own, "row", axis=0)], slots_all
        else:
            arrays, slots = gather(own, rows), slots_xor
        at = 0
        for eighths in chunks:
            chunk = width * eighths // 8
            sums = product(arrays, after(slots, order), integrals, mask, at, chunk, min(chunk, 512))
            split = cols == 4 and len(chains) == count - 1
            chains.append(Chain(sums.reshape(cols, share, m, chunk), cols, split))
            where.append((part, slice(at, at + chunk)))
            at += chunk
            for edge, chain in enumerate(chains[: -cols : -1]):
                order = chain.advance(edge, order)
    for late in range(1, cols - 1):
        for edge in range(late, cols - 1):
            if edge - late < len(chains):
                order = chains[late - edge - 1].advance(edge, order)

    outs = {}
    for (part, span), chain in zip(where, chains):
        denom = virtual_energy[None, None, span] - occupied[:, part]
        value = (driving[:, part, span].astype(jnp.float32) + chain.total()) / denom
        outs.setdefault(part.start, []).append(value)
    outs = [jnp.concatenate(parts, axis=2) for parts in outs.values()]
    return jnp.concatenate(outs, axis=1).reshape(share * local, width)


def solution(mesh):
    in_specs = (
        P("row", "col"),
        P("col", "row"),
        P("col", "row"),
        P("col", "row"),
        P("col"),
        P("row"),
    )
    fn = functools.partial(shards, mesh.shape["row"], mesh.shape["col"])
    return jax.shard_map(fn, mesh=mesh, in_specs=in_specs, out_specs=P("col", "row"), check_vma=False)
```

```python
import functools
import jax
import jax.numpy as jnp
from jax import lax
from jax.experimental import pallas as pl
from jax.experimental.pallas import tpu as pltpu
from jax.sharding import PartitionSpec as P

MIB = 2**20


def product_kernel(pieces, slot_ref, *refs):
    sources = refs[: len(pieces)]
    integrals_ref, mask_ref, out_ref, rows, masked, sems = refs[len(pieces) :]

    @pl.when(pl.program_id(0) == 0)
    def _():
        copies = []
        for ref, count in zip(sources, pieces):
            for k in range(count):
                g = len(copies)
                source = ref.at[k] if count > 1 else ref
                copies.append(pltpu.make_async_copy(source, rows.at[slot_ref[g]], sems.at[g]))
        for copy in copies:
            copy.start()
        for copy in copies:
            copy.wait()

    tile = masked.shape[0] // mask_ref.shape[0]
    for t in range(mask_ref.shape[0]):
        part = slice(t * tile, (t + 1) * tile)
        masked[part, :] = integrals_ref[part, :] * mask_ref[t : t + 1, :]
    every = rows[...].reshape(rows.shape[0] * rows.shape[1], rows.shape[2])
    total = jnp.dot(every, masked[...], preferred_element_type=jnp.float32)
    out_ref[...] = total.reshape(out_ref.shape)


def product(arrays, slots, integrals, mask, first, width, block):
    m, depth = arrays[0].shape[-2:]
    pieces = [a.shape[0] if a.ndim == 3 else 1 for a in arrays]
    devices, tiles = sum(pieces), mask.shape[0]
    grid_spec = pltpu.PrefetchScalarGridSpec(
        num_scalar_prefetch=1,
        grid=(width // block,),
        in_specs=[pl.BlockSpec(memory_space=pl.ANY)] * len(arrays)
        + [
            pl.BlockSpec((depth, block), lambda n, s: (0, first // block + n)),
            pl.BlockSpec((tiles, block), lambda n, s: (0, first // block + n)),
        ],
        out_specs=pl.BlockSpec((devices, m, block), lambda n, s: (0, 0, n)),
        scratch_shapes=[
            pltpu.VMEM((devices, m, depth), jnp.bfloat16),
            pltpu.VMEM((depth, block), jnp.bfloat16),
            pltpu.SemaphoreType.DMA((devices,)),
        ],
    )
    return pl.pallas_call(
        functools.partial(product_kernel, pieces),
        grid_spec=grid_spec,
        out_shape=jax.ShapeDtypeStruct((devices, m, width), jnp.float32),
        compiler_params=pltpu.CompilerParams(vmem_limit_bytes=56 * MIB),
        cost_estimate=pl.CostEstimate(
            flops=2 * devices * m * depth * width,
            bytes_accessed=2 * depth * width + 4 * devices * m * width,
            transcendentals=0,
        ),
    )(slots, *arrays, integrals, mask)


def gather(own, rows):
    swap = [(i, i ^ 1) for i in range(rows)]
    pieces = [own, lax.ppermute(own, "row", swap)]
    for q in range(2, rows, 2):
        other = lax.ppermute(own, "row", [(i, i ^ q) for i in range(rows)])
        other = after(other, pieces[1:2])
        pieces += [other, lax.ppermute(other, "row", swap)]
    return pieces


def send(values, cols, edge):
    pairs = [(edge, edge + 1), (cols - 1 - edge, cols - 2 - edge)]
    return lax.ppermute(values, "col", pairs)


def after(value, others):
    return lax.optimization_barrier((value, *others))[0]


class Chain:
    def __init__(self, sums, cols, split):
        self.sums, self.cols, self.last = sums, cols, cols - 1
        self.groups = [(s, s + 1) for s in range(cols - 1)] if split else [(0, cols - 1)]
        self.came, self.ends = {}, []

    def advance(self, edge, order):
        last, came = self.last, {}
        for low, high in self.groups:
            at = max(low, edge)
            if at >= high:
                continue
            if edge < self.cols // 2:
                values = self.sums[at:high]
            else:
                values = jnp.flip(self.sums[last - high : last - at], 0)
            if edge:
                first, received = self.came[at - 1]
                received = after(received, order)
                values = values + received[at - 1 - first : high - 1 - first].astype(jnp.float32)
            values = values.astype(jnp.float16)
            order = [values]
            received = send(values, self.cols, edge)
            for k in range(at, high):
                came[k] = (at, received)
        self.came = came
        self.ends.append(received)
        return order

    def total(self):
        total = self.sums[self.last]
        for received in self.ends:
            total = total + received[-1].astype(jnp.float32)
        return total


def plan(local):
    if local == 128:
        return ((16, False, (8,)), (48, True, (4, 4)), (64, True, (4, 4)))
    return ((local, True, (8,)),)


def shards(rows, cols, amplitudes, integrals, tile_mask, driving, occupied_energy, virtual_energy):
    local, depth = amplitudes.shape
    width = integrals.shape[1]
    share = rows // cols
    me, place = lax.axis_index("row"), lax.axis_index("col")
    mask = jnp.repeat(tile_mask.astype(jnp.bfloat16), width // tile_mask.shape[1], axis=1)

    lower = place < cols // 2
    near = jnp.where(lower, place, cols - 1 - place)

    def slot_of(device):
        target = device // share
        target = jnp.where(lower, target, cols - 1 - target)
        return jnp.remainder(2 * cols - 1 + near - target, cols) * share + device % share

    device = jnp.arange(rows, dtype=jnp.int32)
    slots_all, slots_xor = slot_of(device), slot_of(jnp.bitwise_xor(device, me))

    driving = driving.reshape(share, local, width)
    occupied = occupied_energy.reshape(share, local, 1)
    layout = plan(local)
    count = sum(len(chunks) for _, _, chunks in layout)
    chains, order, offset, where = [], [], 0, []
    for m, whole, chunks in layout:
        part = slice(offset, offset + m)
        offset += m
        own = amplitudes[part]
        if whole:
            arrays, slots = [lax.all_gather(own, "row", axis=0)], slots_all
        else:
            arrays, slots = gather(own, rows), slots_xor
        at = 0
        for eighths in chunks:
            chunk = width * eighths // 8
            sums = product(arrays, after(slots, order), integrals, mask, at, chunk, min(chunk, 512))
            split = cols == 4 and len(chains) == count - 1
            chains.append(Chain(sums.reshape(cols, share, m, chunk), cols, split))
            where.append((part, slice(at, at + chunk)))
            at += chunk
            for edge, chain in enumerate(chains[: -cols : -1]):
                order = chain.advance(edge, order)
    for late in range(1, cols - 1):
        for edge in range(late, cols - 1):
            if edge - late < len(chains):
                order = chains[late - edge - 1].advance(edge, order)

    outs = {}
    for (part, span), chain in zip(where, chains):
        denom = virtual_energy[None, None, span] - occupied[:, part]
        value = (driving[:, part, span].astype(jnp.float32) + chain.total()) / denom
        outs.setdefault(part.start, []).append(value)
    outs = [jnp.concatenate(parts, axis=2) for parts in outs.values()]
    return jnp.concatenate(outs, axis=1).reshape(share * local, width)


def solution(mesh):
    in_specs = (
        P("row", "col"),
        P("col", "row"),
        P("col", "row"),
        P("col", "row"),
        P("col"),
        P("row"),
    )
    fn = functools.partial(shards, mesh.shape["row"], mesh.shape["col"])
    return jax.shard_map(fn, mesh=mesh, in_specs=in_specs, out_specs=P("col", "row"), check_vma=False)
```
